256 devices in a mesh: ctx: 16 (over z_hi, y), ch: 16 (over x, z_lo, core).
Axes of the slice: x: 4, y: 4, z: 8 (z_hi: 4, z_lo: 2; z = z_hi * 2 + z_lo), core: 2. Of those that a mesh axis runs over, the one named last changes fastest.
Arguments:
- prefix_values: bfloat16 [4096, 4096], P('ctx', 'ch'), may hold values from -6 to 6
- inner_gate: bfloat16 [4096, 4096], P('ctx', 'ch'), may hold values from -6 to 6
- outer_gate: bfloat16 [4096, 4096], P('ctx', 'ch'), may hold values from -6 to 6
- inner_filter: bfloat16 [4096, 4096], P('ctx', 'ch'), may hold values from -0.09375 to 0.09375
- outer_filter: bfloat16 [4096, 4096], P('ctx', 'ch'), may hold values from -0.09375 to 0.09375
- response_values: bfloat16 [16, 1024, 4096], P('ctx', None, 'ch'), may hold values from -6 to 6
- response_inner: bfloat16 [16, 1024, 4096], P('ctx', None, 'ch'), may hold values from -6 to 6
- response_outer: bfloat16 [16, 1024, 4096], P('ctx', None, 'ch'), may hold values from -6 to 6
- lengths: int32 [16], P('ctx'), may hold values from 1 to 1024, 12288 in all
- readout: float32 [4096], P('ch'), may hold values from -1 to 1
Outputs:
- prefix_output: bfloat16 [4096, 4096], P('ctx', 'ch')
- response_output: bfloat16 [16, 1024, 4096], P('ctx', None, 'ch')
- scores: float32 [16], P('ctx')
The draws below stay inside these ranges and needn't reach their ends.
Inputs may be any that keep to these rules, and one draw needn't show every extreme that they name: `lengths`: a response's valid tokens are its first ones; some response has all 1024.
All inputs are finite; a program needn't handle non-finite values. No bound on the sum of `lengths` on one device may be relied on, other than what follows from the above.
Results may differ from the reference program's by a relative error of at most 0.0049.
Values may be sent and summed in bfloat16 or wider, within the bound.
A program may use at most 128 MiB of HBM per device.

```python
import math
import jax
import jax.numpy as jnp
import numpy as np
from jax import lax

C = 4096
RLEN = 1024
PREFIX = 4096
RESP = 16


def draw_readout(key, part):
    position = jnp.arange(C, dtype=jnp.int32).astype(jnp.float32) / max(C - 1, 1)
    base = jax.random.truncated_normal(key, -3.0, 3.0, (C,), jnp.float32)
    rising = jnp.exp(jnp.log(3.0) * position)
    return base * rising / math.sqrt(C)


def steps_of(stream_key, shape, shards, least, high):
    loudness, own = 1.0, jax.random.fold_in(stream_key, 6)
    for axis_at, blocks in shards:
        draws = jnp.exp(jax.random.uniform(jax.random.fold_in(own, axis_at), (blocks,), jnp.float32, least / len(shards), high / len(shards)))
        loudness = loudness * jnp.repeat(draws, shape[axis_at] // blocks).reshape([-1 if axis == axis_at else 1 for axis in range(len(shape))])
    return loudness


def split_up(count, total, reach, skew):
    weights = [(1 << 20) // math.isqrt(grade ** skew) + 1 for grade in range(2, count + 1)]
    surplus, given = total - reach - (count - 1), [1] * (count - 1)
    while surplus > 0:
        candidates = [i for i in range(count - 1) if given[i] < reach]
        mass, budget = sum([weights[i] for i in candidates]), surplus
        for i in candidates:
            extra = min(reach - given[i], max(1, budget * weights[i] // mass), surplus)
            given[i] = given[i] + extra
            surplus = surplus - extra
    return np.array([reach] + given)


def ragged(key, number_of, total, bound, slope):
    if number_of == 2:
        one = jax.random.randint(key, (), max(1, total - bound), min(bound, total - 1) + 1)
        return jnp.stack([one, total - one])
    tallies = jnp.asarray(split_up(number_of, total, bound, slope), jnp.int32)
    twos = (number_of - 1) // 2
    source_of, receiver = tallies[1:1 + 2 * twos:2], tallies[2:2 + 2 * twos:2]
    room = jnp.minimum(source_of - 1, bound - receiver)
    moved = jax.random.randint(jax.random.fold_in(key, 1), (twos,), 0, 1 << 20) % (room + 1)
    tallies = tallies.at[1:1 + 2 * twos:2].set(source_of - moved).at[2:2 + 2 * twos:2].set(receiver + moved)
    return tallies[jax.random.permutation(jax.random.fold_in(key, 2), number_of)]


def normal_values(stream_key, extent, deviation, bound, pieces=(), kind=jnp.bfloat16):
    loudness = steps_of(stream_key, extent, pieces, -0.22, 0.18) if pieces else 1.0
    entries = jax.random.normal(stream_key, extent, jnp.float32) * deviation * loudness
    return jnp.minimum(jnp.maximum(entries, -bound), bound).astype(kind)


def setup_inputs(seed: int = 0) -> dict:
    key_list = jax.random.split(jax.random.key(seed), 11)
    prefix_values = normal_values(key_list[0], (PREFIX, C), 1.0, 6.0, ((0, 16), (1, 16)))
    inner_gate = normal_values(key_list[1], (PREFIX, C), 1.0, 6.0, ((0, 16), (1, 16)))
    outer_gate = normal_values(key_list[2], (PREFIX, C), 1.0, 6.0, ((0, 16), (1, 16)))
    inner_filter = normal_values(key_list[3], (PREFIX, C), PREFIX ** -0.5, 0.09375, ((0, 16), (1, 16)))
    outer_filter = normal_values(key_list[4], (PREFIX, C), PREFIX ** -0.5, 0.09375, ((0, 16), (1, 16)))
    response_values = normal_values(key_list[5], (RESP, RLEN, C), 1.0, 6.0, ((0, 16), (2, 16)))
    response_inner = normal_values(key_list[6], (RESP, RLEN, C), 1.0, 6.0, ((0, 16), (2, 16)))
    response_outer = normal_values(key_list[7], (RESP, RLEN, C), 1.0, 6.0, ((0, 16), (2, 16)))
    lengths = ragged(key_list[8], RESP, RESP * RLEN * 3 // 4, RLEN, 0).astype(jnp.int32)
    readout = draw_readout(jax.random.fold_in(key_list[10], 71), 0)
    return {"prefix_values": prefix_values, "inner_gate": inner_gate, "outer_gate": outer_gate, "inner_filter": inner_filter, "outer_filter": outer_filter, "response_values": response_values, "response_inner": response_inner, "response_outer": response_outer, "lengths": lengths, "readout": readout}


def causal_pieces(signal, filter_taps, length):
    spectrum = jnp.fft.rfft(signal.astype(jnp.float32), n=length, axis=0) * jnp.fft.rfft(filter_taps.astype(jnp.float32), n=length, axis=0)
    return jnp.fft.irfft(spectrum, n=length, axis=0)


def blocked_convolution(signal, filter_taps, keep_rows):
    row_count = signal.shape[0]
    columns = signal.shape[1]
    block_size = math.gcd(256, columns)
    groups = columns // block_size
    signal_blocks = signal.reshape(row_count, groups, block_size).transpose(1, 0, 2)
    taps_blocks = filter_taps.reshape(row_count, groups, block_size).transpose(1, 0, 2)

    def single(couple):
        return causal_pieces(couple[0], couple[1], 2 * row_count)[:keep_rows]

    result = lax.map(single, (signal_blocks, taps_blocks))
    return result.transpose(1, 0, 2).reshape(keep_rows, columns)


def reference(prefix_values, inner_gate, outer_gate, inner_filter, outer_filter, response_values, response_inner, response_outer, lengths, readout):
    keep_rows = PREFIX + RLEN
    conv_one = blocked_convolution(prefix_values, inner_filter, keep_rows)
    gated_one = (inner_gate.astype(jnp.float32) * conv_one[:PREFIX]).astype(jnp.bfloat16)
    conv_two = blocked_convolution(gated_one, outer_filter, keep_rows)
    prefix_output = (outer_gate.astype(jnp.float32) * conv_two[:PREFIX]).astype(jnp.bfloat16)
    tail_one = conv_one[PREFIX:]
    tail_two = conv_two[PREFIX:]

    def respond(members):
        values, inner, outer = members
        own_one = blocked_convolution(values, inner_filter[:RLEN], RLEN)
        gated = (inner.astype(jnp.float32) * (tail_one + own_one)).astype(jnp.bfloat16)
        own_two = blocked_convolution(gated, outer_filter[:RLEN], RLEN)
        return outer.astype(jnp.float32) * (tail_two + own_two)

    ungated = lax.map(respond, (response_values, response_inner, response_outer))
    in_range = jnp.arange(RLEN, dtype=jnp.int32)[None, :] < lengths[:, None]
    response_output = jnp.where(in_range[:, :, None], ungated, 0.0).astype(jnp.bfloat16)
    projection = jnp.sum(response_output.astype(jnp.float32) * readout[None, None, :], axis=2)
    squares = jnp.where(in_range, projection * projection, 0.0)
    scores = jnp.sum(squares, axis=1) / lengths.astype(jnp.float32)
    return prefix_output, response_output, scores
```

```python
import functools

import jax
import jax.numpy as jnp
import ml_dtypes
import numpy as np
from jax import lax
from jax.experimental import pallas as pl
from jax.experimental.pallas import tpu as pltpu
from jax.sharding import PartitionSpec as P

BLK = 256
NCTX = 16
NY = 4
NZ = NCTX // NY
OWN = BLK // NCTX
RBLK = 4
NOUT = NCTX + RBLK
MESH = pl.DeviceIdType.MESH
F32 = jnp.float32
BF16 = jnp.bfloat16


def dft_tables():
    k = np.arange(BLK, dtype=np.int64)[:, None]
    n = np.arange(BLK, dtype=np.int64)[None, :]
    angle = ((2 * k + 1) * n % (4 * BLK)).astype(np.float64) * (np.pi / (2 * BLK))
    table = np.concatenate([np.cos(angle), -np.sin(angle)], axis=0)
    high = table.astype(ml_dtypes.bfloat16)
    low = (table - high.astype(np.float64)).astype(ml_dtypes.bfloat16)
    return high, low, np.ascontiguousarray(high.T), np.ascontiguousarray(low.T)


def dot(a, b):
    return jnp.dot(a, b, preferred_element_type=F32)


def dot_nt(a, b):
    return lax.dot_general(a, b, (((1,), (1,)), ((), ())), preferred_element_type=F32)


def split(value):
    high = value.astype(BF16)
    low = (value - high.astype(F32)).astype(BF16)
    return high, low


def kernel(
    nch,
    x_ref,
    g1_ref,
    g2_ref,
    h1_ref,
    h2_ref,
    v_ref,
    ri_ref,
    ro_ref,
    len_ref,
    rd_ref,
    f_hi,
    f_lo,
    ft_hi,
    ft_lo,
    po_ref,
    out_ref,
    sc_ref,
    send_in,
    recv_in,
    xr_ref,
    xi_ref,
    hr_ref,
    hi_ref,
    q_ref,
    gath,
    back_send,
    back_recv,
    vs_ref,
    hs_ref,
    q_hi,
    q_lo,
    p_send,
    p_recv,
    in_send_sem,
    in_recv_sem,
    gz_send_sem,
    gz_recv_sem,
    gy_send_sem,
    gy_recv_sem,
    back_send_sem,
    back_recv_sem,
    p_send_sem,
    p_recv_sem,
):
    me = lax.axis_index("ctx")
    mc = lax.axis_index("ch")
    zh = me // NY
    yy = lax.rem(me, NY)

    def loop(low, high, body):
        def step(i, carry):
            body(i)
            return carry

        lax.fori_loop(low, high, step, 0)

    def ctx_peer(k):
        return lax.rem(me + k, NCTX)

    barrier = pltpu.get_barrier_semaphore()
    loop(
        1,
        NCTX,
        lambda k: pl.semaphore_signal(
            barrier, inc=1, device_id={"ctx": ctx_peer(k)}, device_id_type=MESH
        ),
    )
    if nch > 1:
        loop(
            1,
            nch,
            lambda k: pl.semaphore_signal(
                barrier, inc=1, device_id={"ch": lax.rem(mc + k, nch)}, device_id_type=MESH
            ),
        )

    mine = pl.ds(pl.multiple_of(me * OWN, OWN), OWN)
    stages = ((0, 2), (2, 2), (4, 1))

    def in_copy(stage, k):
        first, count = stages[stage]
        peer = ctx_peer(k)
        rows = pl.ds(pl.multiple_of(peer * OWN, OWN), OWN)
        return pltpu.make_async_remote_copy(
            src_ref=send_in.at[pl.ds(first, count), rows, :],
            dst_ref=recv_in.at[pl.ds(first, count), mine, :],
            send_sem=in_send_sem.at[stage, k],
            recv_sem=in_recv_sem.at[stage, k],
            device_id={"ctx": peer},
            device_id_type=MESH,
        )

    def pack(slot, ref):
        send_in[slot] = jnp.transpose(ref[...])
        recv_in[slot, mine, :] = send_in[slot, mine, :]

    pack(0, x_ref)
    pack(1, h1_ref)
    pl.semaphore_wait(barrier, NCTX - 1 + nch - 1)
    loop(1, NCTX, lambda k: in_copy(0, k).start())
    pack(2, g1_ref)
    pack(3, h2_ref)
    loop(1, NCTX, lambda k: in_copy(1, k).start())
    pack(4, g2_ref)
    loop(1, NCTX, lambda k: in_copy(2, k).start())

    rows_y = pl.ds(pl.multiple_of(yy * OWN, OWN), OWN)

    def gz_copy(kind, k):
        part = gath.at[kind, :, zh, rows_y, :]
        return pltpu.make_async_remote_copy(
            src_ref=part,
            dst_ref=part,
            send_sem=gz_send_sem.at[kind, k],
            recv_sem=gz_recv_sem.at[kind, k],
            device_id={"ctx": lax.rem(zh + k, NZ) * NY + yy},
            device_id_type=MESH,
        )

    def gy_copy(kind, k):
        part = gath.at[kind, :, :, rows_y, :]
        return pltpu.make_async_remote_copy(
            src_ref=part,
            dst_ref=part,
            send_sem=gy_send_sem.at[kind, k],
            recv_sem=gy_recv_sem.at[kind, k],
            device_id={"ctx": zh * NY + lax.rem(yy + k, NY)},
            device_id_type=MESH,
        )

    def share_z(kind, rows):
        for b in range(RBLK):
            gath[kind, b, zh, rows_y, :] = rows[b * OWN : (b + 1) * OWN]
        loop(1, NZ, lambda k: gz_copy(kind, k).start())

    def share_y(kind):
        loop(1, NZ, lambda k: gz_copy(kind, k).wait_recv())
        loop(1, NY, lambda k: gy_copy(kind, k).start())

    def shared(kind):
        loop(1, NY, lambda k: gy_copy(kind, k).wait_recv())

    def rows_spectrum(rows):
        return dot(rows, ft_hi[...]) + dot(rows, ft_lo[...])

    lane_sign = 1.0 - 2.0 * lax.rem(
        lax.broadcasted_iota(jnp.int32, (OWN, BLK), 1), 2
    ).astype(F32)

    def set_taps(rows):
        s = rows_spectrum(rows)
        for j in range(NCTX):
            hr_ref[j] = s[j * OWN : (j + 1) * OWN, :BLK]
            hi_ref[j] = s[j * OWN : (j + 1) * OWN, BLK:]

    def owner_convolution(rows):
        s = rows_spectrum(rows)
        prev = None
        for m in range(NCTX + 1):
            now = None
            if m < NCTX:
                now = (s[m * OWN : (m + 1) * OWN, :BLK], s[m * OWN : (m + 1) * OWN, BLK:])
            if prev is None:
                real, imag = now
            else:
                real, imag = -lane_sign * prev[1], lane_sign * prev[0]
                if now is not None:
                    real, imag = now[0] + real, now[1] + imag
            xr_ref[m] = real
            xi_ref[m] = imag
            prev = now
        for i in range(NOUT):
            real = imag = None
            for m in range(max(0, i - NCTX + 1), min(i, NCTX) + 1):
                xr, xi, hr, hi = xr_ref[m], xi_ref[m], hr_ref[i - m], hi_ref[i - m]
                pr = xr * hr - xi * hi
                pi = xr * hi + xi * hr
                real = pr if real is None else real + pr
                imag = pi if imag is None else imag + pi
            q_ref[i * OWN : (i + 1) * OWN, :BLK] = real
            q_ref[i * OWN : (i + 1) * OWN, BLK:] = imag
        high, low = split(q_ref[...])
        fh, fl = f_hi[...], f_lo[...]
        return (dot(high, fh) + dot(low, fh) + dot(high, fl)) * (1.0 / BLK)

    def columns_spectrum(store, block, nt):
        def one(b):
            a = block(b)
            mul = dot_nt if nt else dot
            store[b] = mul(f_hi[...], a) + mul(f_lo[...], a)

        loop(0, RBLK, one)

    chunk = 16
    row_sign = 1.0 - 2.0 * lax.rem(
        lax.broadcasted_iota(jnp.int32, (chunk, BLK), 0), 2
    ).astype(F32)

    def response_products():
        def one(n):
            at = pl.ds(pl.multiple_of(n * chunk, chunk), chunk)
            at_i = pl.ds(pl.multiple_of(BLK + n * chunk, chunk), chunk)
            sig = []
            prev = None
            for m in range(RBLK):
                now = (vs_ref[m, at, :], vs_ref[m, at_i, :])
                if prev is None:
                    sig.append(now)
                else:
                    sig.append((now[0] - row_sign * prev[1], now[1] + row_sign * prev[0]))
                prev = now
            tap = [(hs_ref[j, at, :], hs_ref[j, at_i, :]) for j in range(RBLK)]
            for i in range(RBLK):
                real = imag = None
                for m in range(i + 1):
                    (xr, xi), (hr, hi) = sig[m], tap[i - m]
                    pr = xr * hr - xi * hi
                    pi = xr * hi + xi * hr
                    real = pr if real is None else real + pr
                    imag = pi if imag is None else imag + pi
                q_hi[i, at, :], q_lo[i, at, :] = split(real * (1.0 / BLK))
                q_hi[i, at_i, :], q_lo[i, at_i, :] = split(imag * (1.0 / BLK))

        loop(0, BLK // chunk, one)

    def response_block(b):
        high, low = q_hi[b], q_lo[b]
        return dot(ft_hi[...], high) + dot(ft_hi[...], low) + dot(ft_lo[...], high)

    def tokens(b):
        return pl.ds(pl.multiple_of(b * BLK, BLK), BLK)

    def gathered(kind, b):
        return gath[kind, b].reshape(BLK, BLK)

    columns_spectrum(vs_ref, lambda b: v_ref[tokens(b), :], False)

    loop(1, NCTX, lambda k: in_copy(0, k).wait_recv())
    share_z(0, recv_in[1, : RBLK * OWN, :])
    set_taps(recv_in[1])
    conv = owner_convolution(recv_in[0])
    share_z(1, conv[BLK:].astype(BF16))
    share_y(0)
    loop(1, NCTX, lambda k: in_copy(1, k).wait_recv())
    share_z(2, recv_in[3, : RBLK * OWN, :])
    set_taps(recv_in[3])
    gated = (recv_in[2].astype(F32) * conv[:BLK]).astype(BF16)
    conv = owner_convolution(gated)
    share_z(3, conv[BLK:].astype(BF16))
    share_y(1)
    share_y(2)

    loop(1, NCTX, lambda k: in_copy(2, k).wait_recv())
    back_send[...] = (recv_in[4].astype(F32) * conv[:BLK]).astype(BF16)
    back_recv[mine, :] = back_send[mine, :]

    def back_copy(k):
        peer = ctx_peer(k)
        rows = pl.ds(pl.multiple_of(peer * OWN, OWN), OWN)
        return pltpu.make_async_remote_copy(
            src_ref=back_send.at[rows, :],
            dst_ref=back_recv.at[mine, :],
            send_sem=back_send_sem.at[k],
            recv_sem=back_recv_sem.at[k],
            device_id={"ctx": peer},
            device_id_type=MESH,
        )

    share_y(3)
    loop(1, NCTX, lambda k: back_copy(k).start())

    shared(0)
    columns_spectrum(hs_ref, lambda b: gathered(0, b), True)
    response_products()
    shared(1)

    def gate_one(b):
        total = jnp.transpose(gathered(1, b).astype(F32)) + response_block(b)
        gated_block = (ri_ref[tokens(b), :].astype(F32) * total).astype(BF16)
        vs_ref[b] = dot(f_hi[...], gated_block) + dot(f_lo[...], gated_block)

    loop(0, RBLK, gate_one)
    shared(2)
    columns_spectrum(hs_ref, lambda b: gathered(2, b), True)
    response_products()
    shared(3)

    length = len_ref[0]
    weight = jnp.broadcast_to(rd_ref[...], (16, BLK))
    w_hi = weight.astype(BF16).astype(F32)
    w_mid = (weight - w_hi).astype(BF16).astype(F32)
    w_lo = weight - w_hi - w_mid
    w_row = lax.broadcasted_iota(jnp.int32, (16, BLK), 0)
    weight = jnp.where(
        w_row == 0, w_hi, jnp.where(w_row == 1, w_mid, jnp.where(w_row == 2, w_lo, 0.0))
    ).astype(BF16)

    for b in range(RBLK):
        rows = pl.ds(b * BLK, BLK)
        total = jnp.transpose(gathered(3, b).astype(F32)) + response_block(b)
        value = ro_ref[rows, :].astype(F32) * total
        token = lax.broadcasted_iota(jnp.int32, (BLK, BLK), 0) + b * BLK
        block = jnp.where(token < length, value, 0.0).astype(BF16)
        out_ref[rows, :] = block
        part = jnp.sum(dot_nt(weight, block), axis=0, keepdims=True)
        p_send[2 * b : 2 * b + 1, :] = part[:, :128]
        p_send[2 * b + 1 : 2 * b + 2, :] = part[:, 128:]

    def p_copy(k):
        return pltpu.make_async_remote_copy(
            src_ref=p_send,
            dst_ref=p_recv.at[mc],
            send_sem=p_send_sem.at[k],
            recv_sem=p_recv_sem.at[k],
            device_id={"ch": lax.rem(mc + k, nch)},
            device_id_type=MESH,
        )

    p_recv[mc] = p_send[...]
    if nch > 1:
        loop(1, nch, lambda k: p_copy(k).start())

    loop(1, NCTX, lambda k: back_copy(k).wait_recv())
    po_ref[...] = jnp.transpose(back_recv[...])

    if nch > 1:
        loop(1, nch, lambda k: p_copy(k).wait_recv())
    projection = p_recv[0]
    for c in range(1, nch):
        projection = projection + p_recv[c]
    token = (
        lax.broadcasted_iota(jnp.int32, (8, 128), 0) * 128
        + lax.broadcasted_iota(jnp.int32, (8, 128), 1)
    )
    squares = jnp.where(token < length, projection * projection, 0.0)
    sc_ref[0] = jnp.sum(squares) / length.astype(F32)

    for stage in range(len(stages)):
        loop(1, NCTX, lambda k: in_copy(stage, k).wait_send())
    for kind in range(4):
        loop(1, NZ, lambda k: gz_copy(kind, k).wait_send())
        loop(1, NY, lambda k: gy_copy(kind, k).wait_send())
    loop(1, NCTX, lambda k: back_copy(k).wait_send())
    if nch > 1:
        loop(1, nch, lambda k: p_copy(k).wait_send())


def per_device(
    nch,
    prefix_values,
    inner_gate,
    outer_gate,
    inner_filter,
    outer_filter,
    response_values,
    response_inner,
    response_outer,
    lengths,
    readout,
):
    vmem = pl.BlockSpec(memory_space=pltpu.VMEM)
    smem = pl.BlockSpec(memory_space=pltpu.SMEM)
    dma = pltpu.SemaphoreType.DMA
    tokens = RBLK * BLK
    prefix_output, response_output, scores = pl.pallas_call(
        functools.partial(kernel, nch),
        out_shape=(
            jax.ShapeDtypeStruct((BLK, BLK), BF16),
            jax.ShapeDtypeStruct((tokens, BLK), BF16),
            jax.ShapeDtypeStruct((1,), F32),
        ),
        in_specs=[vmem] * 8 + [smem] + [vmem] * 5,
        out_specs=(vmem, vmem, smem),
        scratch_shapes=[
            pltpu.VMEM((5, BLK, BLK), BF16),
            pltpu.VMEM((5, BLK, BLK), BF16),
            pltpu.VMEM((NCTX + 1, OWN, BLK), F32),
            pltpu.VMEM((NCTX + 1, OWN, BLK), F32),
            pltpu.VMEM((NCTX, OWN, BLK), F32),
            pltpu.VMEM((NCTX, OWN, BLK), F32),
            pltpu.VMEM((NOUT * OWN, 2 * BLK), F32),
            pltpu.VMEM((4, RBLK, NZ, NY * OWN, BLK), BF16),
            pltpu.VMEM((BLK, BLK), BF16),
            pltpu.VMEM((BLK, BLK), BF16),
            pltpu.VMEM((RBLK, 2 * BLK, BLK), F32),
            pltpu.VMEM((RBLK, 2 * BLK, BLK), F32),
            pltpu.VMEM((RBLK, 2 * BLK, BLK), BF16),
            pltpu.VMEM((RBLK, 2 * BLK, BLK), BF16),
            pltpu.VMEM((8, 128), F32),
            pltpu.VMEM((nch, 8, 128), F32),
            dma((3, NCTX)),
            dma((3, NCTX)),
            dma((4, NZ)),
            dma((4, NZ)),
            dma((4, NY)),
            dma((4, NY)),
            dma((NCTX,)),
            dma((NCTX,)),
            dma((nch,)),
            dma((nch,)),
        ],
        compiler_params=pltpu.CompilerParams(
            collective_id=0, has_side_effects=True, vmem_limit_bytes=48 * 1024 * 1024
        ),
        cost_estimate=pl.CostEstimate(
            flops=8_000_000_000, bytes_accessed=5_000_000, transcendentals=0
        ),
        name="gated_convolutions",
    )(
        prefix_values,
        inner_gate,
        outer_gate,
        inner_filter,
        outer_filter,
        response_values.reshape(tokens, BLK),
        response_inner.reshape(tokens, BLK),
        response_outer.reshape(tokens, BLK),
        lengths,
        readout.reshape(1, BLK),
        *[jnp.asarray(t) for t in dft_tables()],
    )
    return prefix_output, response_output.reshape(1, tokens, BLK), scores


def solution(mesh):
    in_specs = (
        P("ctx", "ch"),
        P("ctx", "ch"),
        P("ctx", "ch"),
        P("ctx", "ch"),
        P("ctx", "ch"),
        P("ctx", None, "ch"),
        P("ctx", None, "ch"),
        P("ctx", None, "ch"),
        P("ctx"),
        P("ch"),
    )
    out_specs = (P("ctx", "ch"), P("ctx", None, "ch"), P("ctx"))
    return jax.shard_map(
        functools.partial(per_device, mesh.shape["ch"]),
        mesh=mesh,
        in_specs=in_specs,
        out_specs=out_specs,
        check_vma=False,
    )
```

```python
import functools

import jax
import jax.numpy as jnp
import ml_dtypes
import numpy as np
from jax import lax
from jax.experimental import pallas as pl
from jax.experimental.pallas import tpu as pltpu
from jax.sharding import PartitionSpec as P

BLK = 256
NCTX = 16
NY = 4
NZ = NCTX // NY
OWN = BLK // NCTX
RBLK = 4
WORK = BLK // NY
NOUT = NCTX + RBLK
MESH = pl.DeviceIdType.MESH
F32 = jnp.float32
BF16 = jnp.bfloat16


def dft_tables():
    k = np.arange(BLK, dtype=np.int64)[:, None]
    n = np.arange(BLK, dtype=np.int64)[None, :]
    angle = ((2 * k + 1) * n % (4 * BLK)).astype(np.float64) * (np.pi / (2 * BLK))
    table = np.concatenate([np.cos(angle), -np.sin(angle)], axis=0)
    high = table.astype(ml_dtypes.bfloat16)
    low = (table - high.astype(np.float64)).astype(ml_dtypes.bfloat16)
    return high, low, np.ascontiguousarray(high.T), np.ascontiguousarray(low.T)


def dot(a, b):
    return jnp.dot(a, b, preferred_element_type=F32)


def split(value):
    high = value.astype(BF16)
    low = (value - high.astype(F32)).astype(BF16)
    return high, low


def kernel(
    nch,
    x_hbm,
    g1_hbm,
    g2_hbm,
    h1_hbm,
    h2_hbm,
    v_hbm,
    ri_hbm,
    ro_hbm,
    len_ref,
    rd_hbm,
    f_hi_hbm,
    f_lo_hbm,
    ft_hi_hbm,
    ft_lo_hbm,
    po_hbm,
    out_hbm,
    sc_ref,
    po_ref,
    out_ref,
    store_sem,
    x_ref,
    g1_ref,
    g2_ref,
    h1_ref,
    h2_ref,
    v_ref,
    ri_ref,
    ro_ref,
    rd_ref,
    f_hi,
    f_lo,
    ft_hi,
    ft_lo,
    load_sem,
    send_in,
    recv_in,
    resp_send,
    resp_recv,
    xr_ref,
    xi_ref,
    hr_ref,
    hi_ref,
    q_ref,
    gath,
    back_send,
    back_recv,
    vs_ref,
    hs_ref,
    q_hi,
    q_lo,
    out_send,
    out_home,
    p_send,
    p_recv,
    in_send_sem,
    in_recv_sem,
    resp_send_sem,
    resp_recv_sem,
    gz_send_sem,
    gz_recv_sem,
    last_send_sem,
    last_recv_sem,
    back_send_sem,
    back_recv_sem,
    out_send_sem,
    out_recv_sem,
    p_send_sem,
    p_recv_sem,
):
    me = lax.axis_index("ctx")
    mc = lax.axis_index("ch")
    zh = me // NY
    yy = lax.rem(me, NY)

    def loop(low, high, body):
        def step(i, carry):
            body(i)
            return carry

        lax.fori_loop(low, high, step, 0)

    def rows_of(index, size):
        return pl.ds(pl.multiple_of(index * size, size), size)

    def ctx_peer(k):
        return lax.rem(me + k, NCTX)

    def y_peer(k):
        return lax.rem(yy + k, NY)

    def group_of(index):
        return lax.rem(index, NY) * NZ + index // NY

    loads = {}
    for index, (source, target) in enumerate(
        (
            (x_hbm, x_ref),
            (h1_hbm, h1_ref),
            (g1_hbm, g1_ref),
            (h2_hbm, h2_ref),
            (v_hbm, v_ref),
            (ri_hbm, ri_ref),
            (ro_hbm, ro_ref),
            (ft_hi_hbm, ft_hi),
            (ft_lo_hbm, ft_lo),
            (f_hi_hbm, f_hi),
            (f_lo_hbm, f_lo),
            (g2_hbm, g2_ref),
            (rd_hbm, rd_ref),
        )
    ):
        loads[id(target)] = pltpu.make_async_copy(source, target, load_sem.at[index])
        loads[id(target)].start()

    def loaded(*refs):
        for ref in refs:
            loads[id(ref)].wait()

    barrier = pltpu.get_barrier_semaphore()
    loop(
        1,
        NCTX,
        lambda k: pl.semaphore_signal(
            barrier, inc=1, device_id={"ctx": ctx_peer(k)}, device_id_type=MESH
        ),
    )
    if nch > 1:
        loop(
            1,
            nch,
            lambda k: pl.semaphore_signal(
                barrier, inc=1, device_id={"ch": lax.rem(mc + k, nch)}, device_id_type=MESH
            ),
        )

    mine = rows_of(me, OWN)
    my_group = rows_of(group_of(me), OWN)

    def in_copy(stage, k):
        peer = ctx_peer(k)
        return pltpu.make_async_remote_copy(
            src_ref=send_in.at[pl.ds(2 * stage, 2), rows_of(group_of(peer), OWN), :],
            dst_ref=recv_in.at[pl.ds(2 * stage, 2), mine, :],
            send_sem=in_send_sem.at[stage, k],
            recv_sem=in_recv_sem.at[stage, k],
            device_id={"ctx": peer},
            device_id_type=MESH,
        )

    def pack(slot, ref):
        loaded(ref)
        send_in[slot] = jnp.transpose(ref[...])
        recv_in[slot, mine, :] = send_in[slot, my_group, :]

    def resp_copy(which, k):
        peer = y_peer(k)
        return pltpu.make_async_remote_copy(
            src_ref=resp_send.at[which, rows_of(peer, WORK), :],
            dst_ref=resp_recv.at[which, yy],
            send_sem=resp_send_sem.at[which, k],
            recv_sem=resp_recv_sem.at[which, k],
            device_id={"ctx": zh * NY + peer},
            device_id_type=MESH,
        )

    def turn(which, ref):
        loaded(ref)
        for b in range(RBLK):
            at = slice(b * BLK, (b + 1) * BLK)
            resp_send[which, :, at] = jnp.transpose(ref[at, :])

    def send_response(which, ref):
        turn(which, ref)
        loop(1, NY, lambda k: resp_copy(which, k).start())
        resp_recv[which, yy] = resp_send[which, rows_of(yy, WORK), :]

    def have_response(which):
        loop(1, NY, lambda k: resp_copy(which, k).wait_recv())

    def response(which, b):
        return resp_recv[which, :, :, b * BLK : (b + 1) * BLK].reshape(BLK, BLK)

    def z_index(step):
        return lax.rem(zh + step, NZ)

    def gz_copy(kind, k):
        part = gath.at[kind, :, zh]
        return pltpu.make_async_remote_copy(
            src_ref=part,
            dst_ref=part,
            send_sem=gz_send_sem.at[kind, k],
            recv_sem=gz_recv_sem.at[kind, k],
            device_id={"ctx": z_index(k) * NY + yy},
            device_id_type=MESH,
        )

    def last_copy(b, k):
        part = gath.at[3, b, zh]
        return pltpu.make_async_remote_copy(
            src_ref=part,
            dst_ref=part,
            send_sem=last_send_sem.at[b, k],
            recv_sem=last_recv_sem.at[b, k],
            device_id={"ctx": z_index(k) * NY + yy},
            device_id_type=MESH,
        )

    def store_rows(kind, rows):
        for b in range(RBLK):
            gath[kind, b, zh] = rows[b * OWN : (b + 1) * OWN]

    def share(kind, rows):
        store_rows(kind, rows)
        loop(1, NZ, lambda k: gz_copy(kind, k).start())

    def shared(kind):
        loop(1, NZ, lambda k: gz_copy(kind, k).wait_recv())

    def share_last(rows):
        store_rows(3, rows)
        for b in range(RBLK):
            loop(1, NZ, lambda k: last_copy(b, k).start())

    def tail(kind, b):
        rows = gath[kind, b].astype(F32).reshape(WORK, BLK)
        return jnp.concatenate([rows] * NY, axis=0)

    def spectrum(rows):
        return dot(rows, ft_hi[...]) + dot(rows, ft_lo[...])

    def inverse(high, low):
        return dot(high, f_hi[...]) + dot(low, f_hi[...]) + dot(high, f_lo[...])

    sign = 1.0 - 2.0 * lax.rem(lax.broadcasted_iota(jnp.int32, (OWN, BLK), 1), 2).astype(F32)

    def set_taps(rows):
        s = spectrum(rows)
        for j in range(NCTX):
            hr_ref[j] = s[j * OWN : (j + 1) * OWN, :BLK]
            hi_ref[j] = s[j * OWN : (j + 1) * OWN, BLK:]

    def owner_convolution(rows):
        s = spectrum(rows)
        prev = None
        for m in range(NCTX + 1):
            now = None
            if m < NCTX:
                now = (s[m * OWN : (m + 1) * OWN, :BLK], s[m * OWN : (m + 1) * OWN, BLK:])
            if prev is None:
                real, imag = now
            else:
                real, imag = -sign * prev[1], sign * prev[0]
                if now is not None:
                    real, imag = now[0] + real, now[1] + imag
            xr_ref[m] = real
            xi_ref[m] = imag
            prev = now
        for i in range(NOUT):
            real = imag = None
            for m in range(max(0, i - NCTX + 1), min(i, NCTX) + 1):
                xr, xi, hr, hi = xr_ref[m], xi_ref[m], hr_ref[i - m], hi_ref[i - m]
                pr = xr * hr - xi * hi
                pi = xr * hi + xi * hr
                real = pr if real is None else real + pr
                imag = pi if imag is None else imag + pi
            q_ref[i * OWN : (i + 1) * OWN, :BLK] = real
            q_ref[i * OWN : (i + 1) * OWN, BLK:] = imag
        return inverse(*split(q_ref[...])) * (1.0 / BLK)

    def head_spectrum(kind):
        hs_ref[...] = spectrum(gath[kind].reshape(RBLK * WORK, BLK))

    def response_products(blocks):
        def one(n):
            at = rows_of(n, OWN)
            tap_row = lax.rem(n, NZ) * OWN
            sig = []
            prev = None
            for m in range(blocks[-1] + 1):
                now = (vs_ref[m, at, :BLK], vs_ref[m, at, BLK:])
                if prev is None:
                    sig.append(now)
                else:
                    sig.append((now[0] - sign * prev[1], now[1] + sign * prev[0]))
                prev = now
            tap = []
            for j in range(blocks[-1] + 1):
                rows = pl.ds(pl.multiple_of(j * WORK + tap_row, OWN), OWN)
                tap.append((hs_ref[rows, :BLK], hs_ref[rows, BLK:]))
            for i in blocks:
                real = imag = None
                for m in range(i + 1):
                    (xr, xi), (hr, hi) = sig[m], tap[i - m]
                    pr = xr * hr - xi * hi
                    pi = xr * hi + xi * hr
                    real = pr if real is None else real + pr
                    imag = pi if imag is None else imag + pi
                q_hi[i, at, :BLK], q_lo[i, at, :BLK] = split(real * (1.0 / BLK))
                q_hi[i, at, BLK:], q_lo[i, at, BLK:] = split(imag * (1.0 / BLK))

        loop(0, BLK // OWN, one)

    pack(0, x_ref)
    pack(1, h1_ref)
    pl.semaphore_wait(barrier, NCTX - 1 + nch - 1)
    loop(1, NCTX, lambda k: in_copy(0, k).start())
    pack(2, g1_ref)
    pack(3, h2_ref)
    loop(1, NCTX, lambda k: in_copy(1, k).start())
    send_response(0, v_ref)
    send_response(1, ri_ref)
    turn(2, ro_ref)
    loaded(ft_hi, ft_lo, f_hi, f_lo, g2_ref, rd_ref)

    loop(1, NCTX, lambda k: in_copy(0, k).wait_recv())
    share(0, recv_in[1, : RBLK * OWN, :])
    set_taps(recv_in[1])
    conv = owner_convolution(recv_in[0])
    share(1, conv[BLK:].astype(BF16))

    have_response(0)
    for b in range(RBLK):
        vs_ref[b] = spectrum(response(0, b))

    loop(1, NCTX, lambda k: in_copy(1, k).wait_recv())
    share(2, recv_in[3, : RBLK * OWN, :])
    set_taps(recv_in[3])
    gated = (recv_in[2].astype(F32) * conv[:BLK]).astype(BF16)
    conv = owner_convolution(gated)
    share_last(conv[BLK:].astype(BF16))
    back_send[...] = conv[:BLK].astype(BF16)

    shared(0)
    head_spectrum(0)
    response_products(range(RBLK))
    shared(1)
    have_response(1)
    for b in range(RBLK):
        total = tail(1, b) + inverse(q_hi[b], q_lo[b])
        gated = (response(1, b).astype(F32) * total).astype(BF16)
        vs_ref[b] = spectrum(gated)
    shared(2)
    head_spectrum(2)
    response_products(range(RBLK))

    my_work = rows_of(yy, WORK)

    def out_copy(b, k):
        peer = y_peer(k)
        at = pl.ds(b * BLK, BLK)
        return pltpu.make_async_remote_copy(
            src_ref=out_send.at[peer, :, at],
            dst_ref=out_home.at[my_work, at],
            send_sem=out_send_sem.at[b, k],
            recv_sem=out_recv_sem.at[b, k],
            device_id={"ctx": zh * NY + peer},
            device_id_type=MESH,
        )

    for b in range(RBLK):
        at = slice(b * BLK, (b + 1) * BLK)
        own = inverse(q_hi[b], q_lo[b])
        loop(1, NZ, lambda k: last_copy(b, k).wait_recv())
        out_send[:, :, at] = (tail(3, b) + own).astype(BF16).reshape(NY, WORK, BLK)
        loop(1, NY, lambda k: out_copy(b, k).start())
        out_home[my_work, at] = out_send[yy, :, at]

    def back_copy(k):
        peer = ctx_peer(k)
        return pltpu.make_async_remote_copy(
            src_ref=back_send.at[rows_of(peer, OWN), :],
            dst_ref=back_recv.at[my_group, :],
            send_sem=back_send_sem.at[k],
            recv_sem=back_recv_sem.at[k],
            device_id={"ctx": peer},
            device_id_type=MESH,
        )

    loop(1, NCTX, lambda k: back_copy(k).start())
    back_recv[my_group, :] = back_send[mine, :]

    weight = jnp.broadcast_to(rd_ref[...], (16, BLK))
    w_hi = weight.astype(BF16).astype(F32)
    w_mid = (weight - w_hi).astype(BF16).astype(F32)
    w_lo = weight - w_hi - w_mid
    w_row = lax.broadcasted_iota(jnp.int32, (16, BLK), 0)
    weight = jnp.where(
        w_row == 0, w_hi, jnp.where(w_row == 1, w_mid, jnp.where(w_row == 2, w_lo, 0.0))
    ).astype(BF16)

    for b in range(RBLK):
        at = slice(b * BLK, (b + 1) * BLK)
        loop(1, NY, lambda k: out_copy(b, k).wait_recv())
        value = (resp_send[2, :, at].astype(F32) * out_home[:, at].astype(F32)).astype(BF16)
        resp_send[2, :, at] = value
        part = jnp.sum(dot(weight, value), axis=0, keepdims=True)
        p_send[2 * b : 2 * b + 1, :] = part[:, :128]
        p_send[2 * b + 1 : 2 * b + 2, :] = part[:, 128:]

    def p_copy(k):
        return pltpu.make_async_remote_copy(
            src_ref=p_send,
            dst_ref=p_recv.at[mc],
            send_sem=p_send_sem.at[k],
            recv_sem=p_recv_sem.at[k],
            device_id={"ch": lax.rem(mc + k, nch)},
            device_id_type=MESH,
        )

    if nch > 1:
        loop(1, nch, lambda k: p_copy(k).start())
    p_recv[mc] = p_send[...]

    length = len_ref[0]
    stores = []
    for b in range(RBLK):
        at = slice(b * BLK, (b + 1) * BLK)
        token = lax.broadcasted_iota(jnp.int32, (BLK, BLK), 0) + b * BLK
        value = jnp.transpose(resp_send[2, :, at].astype(F32))
        out_ref[at, :] = jnp.where(token < length, value, 0.0).astype(BF16)
        rows = pl.ds(b * BLK, BLK)
        stores.append(
            pltpu.make_async_copy(out_ref.at[rows, :], out_hbm.at[rows, :], store_sem.at[b])
        )
        stores[-1].start()
    loop(1, NCTX, lambda k: back_copy(k).wait_recv())
    po_ref[...] = (
        g2_ref[...].astype(F32) * jnp.transpose(back_recv[...].astype(F32))
    ).astype(BF16)
    stores.append(pltpu.make_async_copy(po_ref, po_hbm, store_sem.at[RBLK]))
    stores[-1].start()

    for stage in range(2):
        loop(1, NCTX, lambda k: in_copy(stage, k).wait_send())
    for which in range(2):
        loop(1, NY, lambda k: resp_copy(which, k).wait_send())
    for kind in range(3):
        loop(1, NZ, lambda k: gz_copy(kind, k).wait_send())
    for b in range(RBLK):
        loop(1, NZ, lambda k: last_copy(b, k).wait_send())
        loop(1, NY, lambda k: out_copy(b, k).wait_send())
    loop(1, NCTX, lambda k: back_copy(k).wait_send())

    if nch > 1:
        loop(1, nch, lambda k: p_copy(k).wait_recv())
    projection = p_recv[0]
    for c in range(1, nch):
        projection = projection + p_recv[c]
    token = (
        lax.broadcasted_iota(jnp.int32, (8, 128), 0) * 128
        + lax.broadcasted_iota(jnp.int32, (8, 128), 1)
    )
    squares = jnp.where(token < length, projection * projection, 0.0)
    sc_ref[0] = jnp.sum(squares) / length.astype(F32)
    if nch > 1:
        loop(1, nch, lambda k: p_copy(k).wait_send())
    for copy in stores:
        copy.wait()


def place(a_ref, b_ref, a_out, b_out, a_buf, b_buf, sem):
    pairs = [(a_ref, a_buf, a_out)]
    for b in range(RBLK):
        rows = pl.ds(b * BLK, BLK)
        pairs.append((b_ref.at[rows, :], b_buf.at[rows, :], b_out.at[rows, :]))
    loads, stores = [], []
    for n, (source, buffer, target) in enumerate(pairs):
        loads.append(pltpu.make_async_copy(source, buffer, sem.at[0, n]))
        stores.append(pltpu.make_async_copy(buffer, target, sem.at[1, n]))
    for copy in loads:
        copy.start()
    for load, store in zip(loads, stores):
        load.wait()
        store.start()
    for copy in stores:
        copy.wait()


def per_device(
    nch,
    prefix_values,
    inner_gate,
    outer_gate,
    inner_filter,
    outer_filter,
    response_values,
    response_inner,
    response_outer,
    lengths,
    readout,
):
    hbm = pl.BlockSpec(memory_space=pl.ANY)
    smem = pl.BlockSpec(memory_space=pltpu.SMEM)
    dma = pltpu.SemaphoreType.DMA
    tokens = RBLK * BLK
    prefix_output, response_output, scores = pl.pallas_call(
        functools.partial(kernel, nch),
        out_shape=(
            jax.ShapeDtypeStruct((BLK, BLK), BF16),
            jax.ShapeDtypeStruct((tokens, BLK), BF16),
            jax.ShapeDtypeStruct((1,), F32),
        ),
        in_specs=[hbm] * 8 + [smem] + [hbm] * 5,
        out_specs=(hbm, hbm, smem),
        scratch_shapes=[
            pltpu.VMEM((BLK, BLK), BF16),
            pltpu.VMEM((tokens, BLK), BF16),
            dma((RBLK + 1,)),
            *[pltpu.VMEM((BLK, BLK), BF16) for _ in range(5)],
            *[pltpu.VMEM((tokens, BLK), BF16) for _ in range(3)],
            pltpu.VMEM((1, BLK), F32),
            *[pltpu.VMEM((2 * BLK, BLK), BF16) for _ in range(2)],
            *[pltpu.VMEM((BLK, 2 * BLK), BF16) for _ in range(2)],
            dma((13,)),
            pltpu.VMEM((4, BLK, BLK), BF16),
            pltpu.VMEM((4, BLK, BLK), BF16),
            pltpu.VMEM((3, BLK, tokens), BF16),
            pltpu.VMEM((2, NY, WORK, tokens), BF16),
            pltpu.VMEM((NCTX + 1, OWN, BLK), F32),
            pltpu.VMEM((NCTX + 1, OWN, BLK), F32),
            pltpu.VMEM((NCTX, OWN, BLK), F32),
            pltpu.VMEM((NCTX, OWN, BLK), F32),
            pltpu.VMEM((NOUT * OWN, 2 * BLK), F32),
            pltpu.VMEM((4, RBLK, NZ, OWN, BLK), BF16),
            pltpu.VMEM((BLK, BLK), BF16),
            pltpu.VMEM((BLK, BLK), BF16),
            pltpu.VMEM((RBLK, BLK, 2 * BLK), F32),
            pltpu.VMEM((RBLK * WORK, 2 * BLK), F32),
            pltpu.VMEM((RBLK, BLK, 2 * BLK), BF16),
            pltpu.VMEM((RBLK, BLK, 2 * BLK), BF16),
            pltpu.VMEM((NY, WORK, tokens), BF16),
            pltpu.VMEM((BLK, tokens), BF16),
            pltpu.VMEM((8, 128), F32),
            pltpu.VMEM((nch, 8, 128), F32),
            dma((2, NCTX)),
            dma((2, NCTX)),
            dma((2, NY)),
            dma((2, NY)),
            dma((3, NZ)),
            dma((3, NZ)),
            dma((RBLK, NZ)),
            dma((RBLK, NZ)),
            dma((NCTX,)),
            dma((NCTX,)),
            dma((RBLK, NY)),
            dma((RBLK, NY)),
            dma((nch,)),
            dma((nch,)),
        ],
        compiler_params=pltpu.CompilerParams(
            collective_id=0, has_side_effects=True, vmem_limit_bytes=60 * 1024 * 1024
        ),
        cost_estimate=pl.CostEstimate(
            flops=8_000_000_000, bytes_accessed=5_000_000, transcendentals=0
        ),
        name="gated_convolutions",
    )(
        prefix_values,
        inner_gate,
        outer_gate,
        inner_filter,
        outer_filter,
        response_values.reshape(tokens, BLK),
        response_inner.reshape(tokens, BLK),
        response_outer.reshape(tokens, BLK),
        lengths,
        readout.reshape(1, BLK),
        *[jnp.asarray(t) for t in dft_tables()],
    )
    prefix_output, response_output = pl.pallas_call(
        place,
        out_shape=(
            jax.ShapeDtypeStruct((BLK, BLK), BF16),
            jax.ShapeDtypeStruct((tokens, BLK), BF16),
        ),
        in_specs=[hbm] * 2,
        out_specs=(hbm, hbm),
        scratch_shapes=[
            pltpu.VMEM((BLK, BLK), BF16),
            pltpu.VMEM((tokens, BLK), BF16),
            dma((2, RBLK + 1)),
        ],
        compiler_params=pltpu.CompilerParams(vmem_limit_bytes=60 * 1024 * 1024),
        name="place_outputs",
    )(prefix_output, response_output)
    return prefix_output, response_output.reshape(1, tokens, BLK), scores


def solution(mesh):
    in_specs = (
        P("ctx", "ch"),
        P("ctx", "ch"),
        P("ctx", "ch"),
        P("ctx", "ch"),
        P("ctx", "ch"),
        P("ctx", None, "ch"),
        P("ctx", None, "ch"),
        P("ctx", None, "ch"),
        P("ctx"),
        P("ch"),
    )
    out_specs = (P("ctx", "ch"), P("ctx", None, "ch"), P("ctx"))
    return jax.shard_map(
        functools.partial(per_device, mesh.shape["ch"]),
        mesh=mesh,
        in_specs=in_specs,
        out_specs=out_specs,
        check_vma=False,
    )
```

```python
import functools

import jax
import jax.numpy as jnp
import ml_dtypes
import numpy as np
from jax import lax
from jax.experimental import pallas as pl
from jax.experimental.pallas import tpu as pltpu
from jax.sharding import PartitionSpec as P

BLK = 256
NCTX = 16
NY = 4
NZ = NCTX // NY
OWN = BLK // NCTX
RBLK = 4
WORK = BLK // NY
NOUT = NCTX + RBLK
MESH = pl.DeviceIdType.MESH
F32 = jnp.float32
BF16 = jnp.bfloat16


def dft_tables():
    k = np.arange(BLK, dtype=np.int64)[:, None]
    n = np.arange(BLK, dtype=np.int64)[None, :]
    angle = ((2 * k + 1) * n % (4 * BLK)).astype(np.float64) * (np.pi / (2 * BLK))
    table = np.concatenate([np.cos(angle), -np.sin(angle)], axis=0)
    high = table.astype(ml_dtypes.bfloat16)
    low = (table - high.astype(np.float64)).astype(ml_dtypes.bfloat16)
    return high, low, np.ascontiguousarray(high.T), np.ascontiguousarray(low.T)


def dot(a, b):
    return jnp.dot(a, b, preferred_element_type=F32)


def split(value):
    high = value.astype(BF16)
    low = (value - high.astype(F32)).astype(BF16)
    return high, low


def kernel(
    nch,
    x_hbm,
    g1_hbm,
    g2_hbm,
    h1_hbm,
    h2_hbm,
    v_hbm,
    ri_hbm,
    ro_hbm,
    len_ref,
    rd_hbm,
    f_hi_hbm,
    f_lo_hbm,
    ft_hi_hbm,
    ft_lo_hbm,
    po_hbm,
    out_hbm,
    sc_ref,
    po_ref,
    out_ref,
    store_sem,
    x_ref,
    g1_ref,
    g2_ref,
    h1_ref,
    h2_ref,
    v_ref,
    ri_ref,
    ro_ref,
    rd_ref,
    f_hi,
    f_lo,
    ft_hi,
    ft_lo,
    load_sem,
    send_in,
    recv_in,
    resp_send,
    resp_recv,
    xr_ref,
    xi_ref,
    hr_ref,
    hi_ref,
    q_ref,
    gath,
    back_send,
    back_recv,
    vs_ref,
    hs_ref,
    q_hi,
    q_lo,
    out_send,
    out_home,
    part_send,
    part_recv,
    p_send,
    p_recv,
    in_send_sem,
    in_recv_sem,
    resp_send_sem,
    resp_recv_sem,
    gz_send_sem,
    gz_recv_sem,
    last_send_sem,
    last_recv_sem,
    back_send_sem,
    back_recv_sem,
    out_send_sem,
    out_recv_sem,
    part_send_sem,
    part_recv_sem,
    p_send_sem,
    p_recv_sem,
):
    me = lax.axis_index("ctx")
    mc = lax.axis_index("ch")
    zh = me // NY
    yy = lax.rem(me, NY)

    def loop(low, high, body):
        def step(i, carry):
            body(i)
            return carry

        lax.fori_loop(low, high, step, 0)

    def rows_of(index, size):
        return pl.ds(pl.multiple_of(index * size, size), size)

    def ctx_peer(k):
        return lax.rem(me + k, NCTX)

    def y_peer(k):
        return lax.rem(yy + k, NY)

    def group_of(index):
        return lax.rem(index, NY) * NZ + index // NY

    loads = {}
    for index, (source, target) in enumerate(
        (
            (x_hbm, x_ref),
            (h1_hbm, h1_ref),
            (g1_hbm, g1_ref),
            (h2_hbm, h2_ref),
            (v_hbm, v_ref),
            (ri_hbm, ri_ref),
            (ro_hbm, ro_ref),
            (ft_hi_hbm, ft_hi),
            (ft_lo_hbm, ft_lo),
            (f_hi_hbm, f_hi),
            (f_lo_hbm, f_lo),
            (g2_hbm, g2_ref),
            (rd_hbm, rd_ref),
        )
    ):
        loads[id(target)] = pltpu.make_async_copy(source, target, load_sem.at[index])
        loads[id(target)].start()

    def loaded(*refs):
        for ref in refs:
            loads[id(ref)].wait()

    barrier = pltpu.get_barrier_semaphore()
    loop(
        1,
        NCTX,
        lambda k: pl.semaphore_signal(
            barrier, inc=1, device_id={"ctx": ctx_peer(k)}, device_id_type=MESH
        ),
    )
    if nch > 1:
        loop(
            1,
            nch,
            lambda k: pl.semaphore_signal(
                barrier, inc=1, device_id={"ch": lax.rem(mc + k, nch)}, device_id_type=MESH
            ),
        )

    mine = rows_of(me, OWN)
    my_group = rows_of(group_of(me), OWN)

    def in_copy(stage, k):
        peer = ctx_peer(k)
        return pltpu.make_async_remote_copy(
            src_ref=send_in.at[pl.ds(2 * stage, 2), rows_of(group_of(peer), OWN), :],
            dst_ref=recv_in.at[pl.ds(2 * stage, 2), mine, :],
            send_sem=in_send_sem.at[stage, k],
            recv_sem=in_recv_sem.at[stage, k],
            device_id={"ctx": peer},
            device_id_type=MESH,
        )

    def pack(slot, ref):
        loaded(ref)
        send_in[slot] = jnp.transpose(ref[...])
        recv_in[slot, mine, :] = send_in[slot, my_group, :]

    def resp_copy(which, k):
        peer = y_peer(k)
        return pltpu.make_async_remote_copy(
            src_ref=resp_send.at[which, rows_of(peer, WORK), :],
            dst_ref=resp_recv.at[which, yy],
            send_sem=resp_send_sem.at[which, k],
            recv_sem=resp_recv_sem.at[which, k],
            device_id={"ctx": zh * NY + peer},
            device_id_type=MESH,
        )

    def send_response(which, ref):
        loaded(ref)
        for b in range(RBLK):
            at = slice(b * BLK, (b + 1) * BLK)
            resp_send[which, :, at] = jnp.transpose(ref[at, :])
        loop(1, NY, lambda k: resp_copy(which, k).start())
        resp_recv[which, yy] = resp_send[which, rows_of(yy, WORK), :]

    def have_response(which):
        loop(1, NY, lambda k: resp_copy(which, k).wait_recv())

    def response(which, b):
        return resp_recv[which, :, :, b * BLK : (b + 1) * BLK].reshape(BLK, BLK)

    def z_index(step):
        return lax.rem(zh + step, NZ)

    def gz_copy(kind, k):
        part = gath.at[kind, :, zh]
        return pltpu.make_async_remote_copy(
            src_ref=part,
            dst_ref=part,
            send_sem=gz_send_sem.at[kind, k],
            recv_sem=gz_recv_sem.at[kind, k],
            device_id={"ctx": z_index(k) * NY + yy},
            device_id_type=MESH,
        )

    def last_copy(b, k):
        part = gath.at[3, b, zh]
        return pltpu.make_async_remote_copy(
            src_ref=part,
            dst_ref=part,
            send_sem=last_send_sem.at[b, k],
            recv_sem=last_recv_sem.at[b, k],
            device_id={"ctx": z_index(k) * NY + yy},
            device_id_type=MESH,
        )

    def store_rows(kind, rows):
        for b in range(RBLK):
            gath[kind, b, zh] = rows[b * OWN : (b + 1) * OWN]

    def share(kind, rows):
        store_rows(kind, rows)
        loop(1, NZ, lambda k: gz_copy(kind, k).start())

    def shared(kind):
        loop(1, NZ, lambda k: gz_copy(kind, k).wait_recv())

    def share_last(rows):
        store_rows(3, rows)
        for b in range(RBLK):
            loop(1, NZ, lambda k: last_copy(b, k).start())

    def tail(kind, b):
        rows = gath[kind, b].astype(F32).reshape(WORK, BLK)
        return jnp.concatenate([rows] * NY, axis=0)

    def spectrum(rows):
        return dot(rows, ft_hi[...]) + dot(rows, ft_lo[...])

    def inverse(high, low):
        return dot(high, f_hi[...]) + dot(low, f_hi[...]) + dot(high, f_lo[...])

    sign = 1.0 - 2.0 * lax.rem(lax.broadcasted_iota(jnp.int32, (OWN, BLK), 1), 2).astype(F32)

    def set_taps(rows):
        s = spectrum(rows)
        for j in range(NCTX):
            hr_ref[j] = s[j * OWN : (j + 1) * OWN, :BLK]
            hi_ref[j] = s[j * OWN : (j + 1) * OWN, BLK:]

    def owner_convolution(rows):
        s = spectrum(rows)
        prev = None
        for m in range(NCTX + 1):
            now = None
            if m < NCTX:
                now = (s[m * OWN : (m + 1) * OWN, :BLK], s[m * OWN : (m + 1) * OWN, BLK:])
            if prev is None:
                real, imag = now
            else:
                real, imag = -sign * prev[1], sign * prev[0]
                if now is not None:
                    real, imag = now[0] + real, now[1] + imag
            xr_ref[m] = real
            xi_ref[m] = imag
            prev = now
        for i in range(NOUT):
            real = imag = None
            for m in range(max(0, i - NCTX + 1), min(i, NCTX) + 1):
                xr, xi, hr, hi = xr_ref[m], xi_ref[m], hr_ref[i - m], hi_ref[i - m]
                pr = xr * hr - xi * hi
                pi = xr * hi + xi * hr
                real = pr if real is None else real + pr
                imag = pi if imag is None else imag + pi
            q_ref[i * OWN : (i + 1) * OWN, :BLK] = real
            q_ref[i * OWN : (i + 1) * OWN, BLK:] = imag
        return inverse(*split(q_ref[...])) * (1.0 / BLK)

    def head_spectrum(kind):
        hs_ref[...] = spectrum(gath[kind].reshape(RBLK * WORK, BLK))

    def response_products(blocks):
        def one(n):
            at = rows_of(n, OWN)
            tap_row = lax.rem(n, NZ) * OWN
            sig = []
            prev = None
            for m in range(blocks[-1] + 1):
                now = (vs_ref[m, at, :BLK], vs_ref[m, at, BLK:])
                if prev is None:
                    sig.append(now)
                else:
                    sig.append((now[0] - sign * prev[1], now[1] + sign * prev[0]))
                prev = now
            tap = []
            for j in range(blocks[-1] + 1):
                rows = pl.ds(pl.multiple_of(j * WORK + tap_row, OWN), OWN)
                tap.append((hs_ref[rows, :BLK], hs_ref[rows, BLK:]))
            for i in blocks:
                real = imag = None
                for m in range(i + 1):
                    (xr, xi), (hr, hi) = sig[m], tap[i - m]
                    pr = xr * hr - xi * hi
                    pi = xr * hi + xi * hr
                    real = pr if real is None else real + pr
                    imag = pi if imag is None else imag + pi
                q_hi[i, at, :BLK], q_lo[i, at, :BLK] = split(real * (1.0 / BLK))
                q_hi[i, at, BLK:], q_lo[i, at, BLK:] = split(imag * (1.0 / BLK))

        loop(0, BLK // OWN, one)

    pack(0, x_ref)
    pack(1, h1_ref)
    pl.semaphore_wait(barrier, NCTX - 1 + nch - 1)
    loop(1, NCTX, lambda k: in_copy(0, k).start())
    pack(2, g1_ref)
    pack(3, h2_ref)
    loop(1, NCTX, lambda k: in_copy(1, k).start())
    send_response(0, v_ref)
    send_response(1, ri_ref)
    send_response(2, ro_ref)
    loaded(ft_hi, ft_lo, f_hi, f_lo, g2_ref, rd_ref)

    loop(1, NCTX, lambda k: in_copy(0, k).wait_recv())
    share(0, recv_in[1, : RBLK * OWN, :])
    set_taps(recv_in[1])
    conv = owner_convolution(recv_in[0])
    share(1, conv[BLK:].astype(BF16))

    have_response(0)
    for b in range(RBLK):
        vs_ref[b] = spectrum(response(0, b))

    loop(1, NCTX, lambda k: in_copy(1, k).wait_recv())
    share(2, recv_in[3, : RBLK * OWN, :])
    set_taps(recv_in[3])
    gated = (recv_in[2].astype(F32) * conv[:BLK]).astype(BF16)
    conv = owner_convolution(gated)
    share_last(conv[BLK:].astype(BF16))
    back_send[...] = conv[:BLK].astype(BF16)

    shared(0)
    head_spectrum(0)
    response_products(range(RBLK))
    shared(1)
    have_response(1)
    for b in range(RBLK):
        total = tail(1, b) + inverse(q_hi[b], q_lo[b])
        gated = (response(1, b).astype(F32) * total).astype(BF16)
        vs_ref[b] = spectrum(gated)
    shared(2)
    head_spectrum(2)
    response_products(range(RBLK))
    have_response(2)

    lane = lax.broadcasted_iota(jnp.int32, (16, BLK), 1)
    row = lax.broadcasted_iota(jnp.int32, (16, BLK), 0)
    weight = jnp.where(lane // WORK == yy, jnp.broadcast_to(rd_ref[...], (16, BLK)), 0.0)
    weight = weight + pltpu.roll(weight, BLK // 2, 1)
    weight = weight + pltpu.roll(weight, WORK, 1)
    w_hi = weight.astype(BF16).astype(F32)
    w_mid = (weight - w_hi).astype(BF16).astype(F32)
    w_lo = weight - w_hi - w_mid
    term = row // NY
    weight = jnp.where(term == 0, w_hi, jnp.where(term == 1, w_mid, w_lo))
    weight = jnp.where(term < 3, weight, 0.0)
    weight = jnp.where(lax.rem(row, NY) == lane // WORK, weight, 0.0).astype(BF16)

    my_work = rows_of(yy, WORK)

    def out_copy(b, k):
        peer = y_peer(k)
        at = pl.ds(b * BLK, BLK)
        return pltpu.make_async_remote_copy(
            src_ref=out_send.at[peer, :, at],
            dst_ref=out_home.at[my_work, at],
            send_sem=out_send_sem.at[b, k],
            recv_sem=out_recv_sem.at[b, k],
            device_id={"ctx": zh * NY + peer},
            device_id_type=MESH,
        )

    for b in range(RBLK):
        vs_ref[b, :, :BLK] = inverse(q_hi[b], q_lo[b])

    for b in range(RBLK):
        at = slice(b * BLK, (b + 1) * BLK)
        loop(1, NZ, lambda k: last_copy(b, k).wait_recv())
        total = tail(3, b) + vs_ref[b, :, :BLK]
        value = (response(2, b).astype(F32) * total).astype(BF16)
        out_send[:, :, at] = value.reshape(NY, WORK, BLK)
        terms = dot(weight, value)
        part = terms[0:4] + terms[4:8] + terms[8:12]
        for n in range(NY):
            part_send[n, 2 * b : 2 * b + 1, :] = part[n : n + 1, :128]
            part_send[n, 2 * b + 1 : 2 * b + 2, :] = part[n : n + 1, 128:]

    def part_copy(k):
        peer = y_peer(k)
        return pltpu.make_async_remote_copy(
            src_ref=part_send.at[peer],
            dst_ref=part_recv.at[yy],
            send_sem=part_send_sem.at[k],
            recv_sem=part_recv_sem.at[k],
            device_id={"ctx": zh * NY + peer},
            device_id_type=MESH,
        )

    loop(1, NY, lambda k: part_copy(k).start())
    for b in range(RBLK):
        loop(1, NY, lambda k: out_copy(b, k).start())
    part_recv[yy] = part_send[yy]
    out_home[my_work, :] = out_send[yy]

    def p_copy(k):
        return pltpu.make_async_remote_copy(
            src_ref=p_send,
            dst_ref=p_recv.at[mc],
            send_sem=p_send_sem.at[k],
            recv_sem=p_recv_sem.at[k],
            device_id={"ch": lax.rem(mc + k, nch)},
            device_id_type=MESH,
        )

    loop(1, NY, lambda k: part_copy(k).wait_recv())
    p_send[...] = part_recv[0] + part_recv[1] + part_recv[2] + part_recv[3]
    if nch > 1:
        loop(1, nch, lambda k: p_copy(k).start())
    p_recv[mc] = p_send[...]

    def back_copy(k):
        peer = ctx_peer(k)
        return pltpu.make_async_remote_copy(
            src_ref=back_send.at[rows_of(peer, OWN), :],
            dst_ref=back_recv.at[my_group, :],
            send_sem=back_send_sem.at[k],
            recv_sem=back_recv_sem.at[k],
            device_id={"ctx": peer},
            device_id_type=MESH,
        )

    loop(1, NCTX, lambda k: back_copy(k).start())
    back_recv[my_group, :] = back_send[mine, :]

    length = len_ref[0]
    stores = []
    for b in range(RBLK):
        at = slice(b * BLK, (b + 1) * BLK)
        loop(1, NY, lambda k: out_copy(b, k).wait_recv())
        token = lax.broadcasted_iota(jnp.int32, (BLK, BLK), 0) + b * BLK
        value = jnp.transpose(out_home[:, at].astype(F32))
        out_ref[at, :] = jnp.where(token < length, value, 0.0).astype(BF16)
        rows = pl.ds(b * BLK, BLK)
        stores.append(
            pltpu.make_async_copy(out_ref.at[rows, :], out_hbm.at[rows, :], store_sem.at[b])
        )
        stores[-1].start()
    loop(1, NCTX, lambda k: back_copy(k).wait_recv())
    po_ref[...] = (
        g2_ref[...].astype(F32) * jnp.transpose(back_recv[...].astype(F32))
    ).astype(BF16)
    stores.append(pltpu.make_async_copy(po_ref, po_hbm, store_sem.at[RBLK]))
    stores[-1].start()

    for stage in range(2):
        loop(1, NCTX, lambda k: in_copy(stage, k).wait_send())
    for which in range(3):
        loop(1, NY, lambda k: resp_copy(which, k).wait_send())
    for kind in range(3):
        loop(1, NZ, lambda k: gz_copy(kind, k).wait_send())
    for b in range(RBLK):
        loop(1, NZ, lambda k: last_copy(b, k).wait_send())
        loop(1, NY, lambda k: out_copy(b, k).wait_send())
    loop(1, NCTX, lambda k: back_copy(k).wait_send())
    loop(1, NY, lambda k: part_copy(k).wait_send())

    if nch > 1:
        loop(1, nch, lambda k: p_copy(k).wait_recv())
    projection = p_recv[0]
    for c in range(1, nch):
        projection = projection + p_recv[c]
    token = (
        lax.broadcasted_iota(jnp.int32, (8, 128), 0) * 128
        + lax.broadcasted_iota(jnp.int32, (8, 128), 1)
    )
    squares = jnp.where(token < length, projection * projection, 0.0)
    sc_ref[0] = jnp.sum(squares) / length.astype(F32)
    if nch > 1:
        loop(1, nch, lambda k: p_copy(k).wait_send())
    for copy in stores:
        copy.wait()


def place(a_ref, b_ref, a_out, b_out, a_buf, b_buf, sem):
    pairs = [(a_ref, a_buf, a_out)]
    for b in range(RBLK):
        rows = pl.ds(b * BLK, BLK)
        pairs.append((b_ref.at[rows, :], b_buf.at[rows, :], b_out.at[rows, :]))
    loads, stores = [], []
    for n, (source, buffer, target) in enumerate(pairs):
        loads.append(pltpu.make_async_copy(source, buffer, sem.at[0, n]))
        stores.append(pltpu.make_async_copy(buffer, target, sem.at[1, n]))
    for copy in loads:
        copy.start()
    for load, store in zip(loads, stores):
        load.wait()
        store.start()
    for copy in stores:
        copy.wait()


def per_device(
    nch,
    prefix_values,
    inner_gate,
    outer_gate,
    inner_filter,
    outer_filter,
    response_values,
    response_inner,
    response_outer,
    lengths,
    readout,
):
    hbm = pl.BlockSpec(memory_space=pl.ANY)
    smem = pl.BlockSpec(memory_space=pltpu.SMEM)
    dma = pltpu.SemaphoreType.DMA
    tokens = RBLK * BLK
    prefix_output, response_output, scores = pl.pallas_call(
        functools.partial(kernel, nch),
        out_shape=(
            jax.ShapeDtypeStruct((BLK, BLK), BF16),
            jax.ShapeDtypeStruct((tokens, BLK), BF16),
            jax.ShapeDtypeStruct((1,), F32),
        ),
        in_specs=[hbm] * 8 + [smem] + [hbm] * 5,
        out_specs=(hbm, hbm, smem),
        scratch_shapes=[
            pltpu.VMEM((BLK, BLK), BF16),
            pltpu.VMEM((tokens, BLK), BF16),
            dma((RBLK + 1,)),
            *[pltpu.VMEM((BLK, BLK), BF16) for _ in range(5)],
            *[pltpu.VMEM((tokens, BLK), BF16) for _ in range(3)],
            pltpu.VMEM((1, BLK), F32),
            *[pltpu.VMEM((2 * BLK, BLK), BF16) for _ in range(2)],
            *[pltpu.VMEM((BLK, 2 * BLK), BF16) for _ in range(2)],
            dma((13,)),
            pltpu.VMEM((4, BLK, BLK), BF16),
            pltpu.VMEM((4, BLK, BLK), BF16),
            pltpu.VMEM((3, BLK, tokens), BF16),
            pltpu.VMEM((3, NY, WORK, tokens), BF16),
            pltpu.VMEM((NCTX + 1, OWN, BLK), F32),
            pltpu.VMEM((NCTX + 1, OWN, BLK), F32),
            pltpu.VMEM((NCTX, OWN, BLK), F32),
            pltpu.VMEM((NCTX, OWN, BLK), F32),
            pltpu.VMEM((NOUT * OWN, 2 * BLK), F32),
            pltpu.VMEM((4, RBLK, NZ, OWN, BLK), BF16),
            pltpu.VMEM((BLK, BLK), BF16),
            pltpu.VMEM((BLK, BLK), BF16),
            pltpu.VMEM((RBLK, BLK, 2 * BLK), F32),
            pltpu.VMEM((RBLK * WORK, 2 * BLK), F32),
            pltpu.VMEM((RBLK, BLK, 2 * BLK), BF16),
            pltpu.VMEM((RBLK, BLK, 2 * BLK), BF16),
            pltpu.VMEM((NY, WORK, tokens), BF16),
            pltpu.VMEM((BLK, tokens), BF16),
            pltpu.VMEM((NY, 8, 128), F32),
            pltpu.VMEM((NY, 8, 128), F32),
            pltpu.VMEM((8, 128), F32),
            pltpu.VMEM((nch, 8, 128), F32),
            dma((2, NCTX)),
            dma((2, NCTX)),
            dma((3, NY)),
            dma((3, NY)),
            dma((3, NZ)),
            dma((3, NZ)),
            dma((RBLK, NZ)),
            dma((RBLK, NZ)),
            dma((NCTX,)),
            dma((NCTX,)),
            dma((RBLK, NY)),
            dma((RBLK, NY)),
            dma((NY,)),
            dma((NY,)),
            dma((nch,)),
            dma((nch,)),
        ],
        compiler_params=pltpu.CompilerParams(
            collective_id=0, has_side_effects=True, vmem_limit_bytes=60 * 1024 * 1024
        ),
        cost_estimate=pl.CostEstimate(
            flops=8_000_000_000, bytes_accessed=5_000_000, transcendentals=0
        ),
        name="gated_convolutions",
    )(
        prefix_values,
        inner_gate,
        outer_gate,
        inner_filter,
        outer_filter,
        response_values.reshape(tokens, BLK),
        response_inner.reshape(tokens, BLK),
        response_outer.reshape(tokens, BLK),
        lengths,
        readout.reshape(1, BLK),
        *[jnp.asarray(t) for t in dft_tables()],
    )
    prefix_output, response_output = pl.pallas_call(
        place,
        out_shape=(
            jax.ShapeDtypeStruct((BLK, BLK), BF16),
            jax.ShapeDtypeStruct((tokens, BLK), BF16),
        ),
        in_specs=[hbm] * 2,
        out_specs=(hbm, hbm),
        scratch_shapes=[
            pltpu.VMEM((BLK, BLK), BF16),
            pltpu.VMEM((tokens, BLK), BF16),
            dma((2, RBLK + 1)),
        ],
        compiler_params=pltpu.CompilerParams(vmem_limit_bytes=60 * 1024 * 1024),
        name="place_outputs",
    )(prefix_output, response_output)
    return prefix_output, response_output.reshape(1, tokens, BLK), scores


def solution(mesh):
    in_specs = (
        P("ctx", "ch"),
        P("ctx", "ch"),
        P("ctx", "ch"),
        P("ctx", "ch"),
        P("ctx", "ch"),
        P("ctx", None, "ch"),
        P("ctx", None, "ch"),
        P("ctx", None, "ch"),
        P("ctx"),
        P("ch"),
    )
    out_specs = (P("ctx", "ch"), P("ctx", None, "ch"), P("ctx"))
    return jax.shard_map(
        functools.partial(per_device, mesh.shape["ch"]),
        mesh=mesh,
        in_specs=in_specs,
        out_specs=out_specs,
        check_vma=False,
    )
```

```python
import functools

import jax
import jax.numpy as jnp
import ml_dtypes
import numpy as np
from jax import lax
from jax.experimental import pallas as pl
from jax.experimental.pallas import tpu as pltpu
from jax.sharding import PartitionSpec as P

BLK = 256
NCTX = 16
NY = 4
NZ = NCTX // NY
OWN = BLK // NCTX
RBLK = 4
WORK = BLK // NY
NOUT = NCTX + RBLK
MESH = pl.DeviceIdType.MESH
F32 = jnp.float32
BF16 = jnp.bfloat16


def dft_tables():
    k = np.arange(BLK, dtype=np.int64)[:, None]
    n = np.arange(BLK, dtype=np.int64)[None, :]
    angle = ((2 * k + 1) * n % (4 * BLK)).astype(np.float64) * (np.pi / (2 * BLK))
    table = np.concatenate([np.cos(angle), -np.sin(angle)], axis=0)
    high = table.astype(ml_dtypes.bfloat16)
    low = (table - high.astype(np.float64)).astype(ml_dtypes.bfloat16)
    return high, low, np.ascontiguousarray(high.T), np.ascontiguousarray(low.T)


def dot(a, b):
    return jnp.dot(a, b, preferred_element_type=F32)


def split(value):
    high = value.astype(BF16)
    low = (value - high.astype(F32)).astype(BF16)
    return high, low


def kernel(
    nch,
    x_hbm,
    g1_hbm,
    g2_hbm,
    h1_hbm,
    h2_hbm,
    v_hbm,
    ri_hbm,
    ro_hbm,
    len_ref,
    rd_hbm,
    f_hi_hbm,
    f_lo_hbm,
    ft_hi_hbm,
    ft_lo_hbm,
    po_hbm,
    out_hbm,
    sc_ref,
    po_ref,
    out_ref,
    store_sem,
    x_ref,
    g1_ref,
    g2_ref,
    h1_ref,
    h2_ref,
    v_ref,
    ri_ref,
    ro_ref,
    rd_ref,
    f_hi,
    f_lo,
    ft_hi,
    ft_lo,
    load_sem,
    send_in,
    recv_in,
    resp_send,
    resp_recv,
    xr_ref,
    xi_ref,
    hr_ref,
    hi_ref,
    q_ref,
    gath,
    back_send,
    back_recv,
    vs_ref,
    hs_ref,
    q_hi,
    q_lo,
    out_send,
    out_home,
    part_send,
    part_recv,
    p_send,
    p_recv,
    in_send_sem,
    in_recv_sem,
    resp_send_sem,
    resp_recv_sem,
    gz_send_sem,
    gz_recv_sem,
    back_send_sem,
    back_recv_sem,
    out_send_sem,
    out_recv_sem,
    part_send_sem,
    part_recv_sem,
    p_send_sem,
    p_recv_sem,
):
    me = lax.axis_index("ctx")
    mc = lax.axis_index("ch")
    zh = me // NY
    yy = lax.rem(me, NY)

    def loop(low, high, body):
        def step(i, carry):
            body(i)
            return carry

        lax.fori_loop(low, high, step, 0)

    def rows_of(index, size):
        return pl.ds(pl.multiple_of(index * size, size), size)

    def ctx_peer(k):
        return lax.rem(me + k, NCTX)

    def y_peer(k):
        return lax.rem(yy + k, NY)

    def group_of(index):
        return lax.rem(index, NY) * NZ + index // NY

    loads = {}
    for index, (source, target) in enumerate(
        (
            (x_hbm, x_ref),
            (h1_hbm, h1_ref),
            (g1_hbm, g1_ref),
            (h2_hbm, h2_ref),
            (v_hbm, v_ref),
            (ri_hbm, ri_ref),
            (ro_hbm, ro_ref),
            (ft_hi_hbm, ft_hi),
            (ft_lo_hbm, ft_lo),
            (f_hi_hbm, f_hi),
            (f_lo_hbm, f_lo),
            (g2_hbm, g2_ref),
            (rd_hbm, rd_ref),
        )
    ):
        loads[id(target)] = pltpu.make_async_copy(source, target, load_sem.at[index])
        loads[id(target)].start()

    def loaded(*refs):
        for ref in refs:
            loads[id(ref)].wait()

    barrier = pltpu.get_barrier_semaphore()
    loop(
        1,
        NCTX,
        lambda k: pl.semaphore_signal(
            barrier, inc=1, device_id={"ctx": ctx_peer(k)}, device_id_type=MESH
        ),
    )
    if nch > 1:
        loop(
            1,
            nch,
            lambda k: pl.semaphore_signal(
                barrier, inc=1, device_id={"ch": lax.rem(mc + k, nch)}, device_id_type=MESH
            ),
        )

    mine = rows_of(me, OWN)
    my_group = rows_of(group_of(me), OWN)

    def in_copy(stage, k):
        peer = ctx_peer(k)
        return pltpu.make_async_remote_copy(
            src_ref=send_in.at[pl.ds(2 * stage, 2), rows_of(group_of(peer), OWN), :],
            dst_ref=recv_in.at[pl.ds(2 * stage, 2), mine, :],
            send_sem=in_send_sem.at[stage, k],
            recv_sem=in_recv_sem.at[stage, k],
            device_id={"ctx": peer},
            device_id_type=MESH,
        )

    def pack(slot, ref):
        loaded(ref)
        send_in[slot] = jnp.transpose(ref[...])
        recv_in[slot, mine, :] = send_in[slot, my_group, :]

    def resp_copy(which, k):
        peer = y_peer(k)
        return pltpu.make_async_remote_copy(
            src_ref=resp_send.at[which, rows_of(peer, WORK), :],
            dst_ref=resp_recv.at[which, yy],
            send_sem=resp_send_sem.at[which, k],
            recv_sem=resp_recv_sem.at[which, k],
            device_id={"ctx": zh * NY + peer},
            device_id_type=MESH,
        )

    def send_response(which, ref):
        loaded(ref)
        for b in range(RBLK):
            at = slice(b * BLK, (b + 1) * BLK)
            resp_send[which, :, at] = jnp.transpose(ref[at, :])
        loop(1, NY, lambda k: resp_copy(which, k).start())
        resp_recv[which, yy] = resp_send[which, rows_of(yy, WORK), :]

    def have_response(which):
        loop(1, NY, lambda k: resp_copy(which, k).wait_recv())

    def response(which, b):
        return resp_recv[which, :, :, b * BLK : (b + 1) * BLK].reshape(BLK, BLK)

    def z_index(step):
        return lax.rem(zh + step, NZ)

    def gz_copy(kind, k):
        part = gath.at[kind, :, zh]
        return pltpu.make_async_remote_copy(
            src_ref=part,
            dst_ref=part,
            send_sem=gz_send_sem.at[kind, k],
            recv_sem=gz_recv_sem.at[kind, k],
            device_id={"ctx": z_index(k) * NY + yy},
            device_id_type=MESH,
        )

    def store_rows(kind, rows):
        for b in range(RBLK):
            gath[kind, b, zh] = rows[b * OWN : (b + 1) * OWN]

    def share(kind, rows):
        store_rows(kind, rows)
        loop(1, NZ, lambda k: gz_copy(kind, k).start())

    def shared(kind):
        loop(1, NZ, lambda k: gz_copy(kind, k).wait_recv())

    def tail(kind, b):
        rows = gath[kind, b].astype(F32).reshape(WORK, BLK)
        return jnp.concatenate([rows] * NY, axis=0)

    def spectrum(rows):
        return dot(rows, ft_hi[...]) + dot(rows, ft_lo[...])

    def inverse(high, low):
        return dot(high, f_hi[...]) + dot(low, f_hi[...]) + dot(high, f_lo[...])

    sign = 1.0 - 2.0 * lax.rem(lax.broadcasted_iota(jnp.int32, (OWN, BLK), 1), 2).astype(F32)

    def set_taps(rows):
        s = spectrum(rows)
        for j in range(NCTX):
            hr_ref[j] = s[j * OWN : (j + 1) * OWN, :BLK]
            hi_ref[j] = s[j * OWN : (j + 1) * OWN, BLK:]

    def owner_convolution(rows):
        s = spectrum(rows)
        prev = None
        for m in range(NCTX + 1):
            now = None
            if m < NCTX:
                now = (s[m * OWN : (m + 1) * OWN, :BLK], s[m * OWN : (m + 1) * OWN, BLK:])
            if prev is None:
                real, imag = now
            else:
                real, imag = -sign * prev[1], sign * prev[0]
                if now is not None:
                    real, imag = now[0] + real, now[1] + imag
            xr_ref[m] = real
            xi_ref[m] = imag
            prev = now
        for i in range(NOUT):
            real = imag = None
            for m in range(max(0, i - NCTX + 1), min(i, NCTX) + 1):
                xr, xi, hr, hi = xr_ref[m], xi_ref[m], hr_ref[i - m], hi_ref[i - m]
                pr = xr * hr - xi * hi
                pi = xr * hi + xi * hr
                real = pr if real is None else real + pr
                imag = pi if imag is None else imag + pi
            q_ref[i * OWN : (i + 1) * OWN, :BLK] = real
            q_ref[i * OWN : (i + 1) * OWN, BLK:] = imag
        return inverse(*split(q_ref[...])) * (1.0 / BLK)

    def head_spectrum(kind):
        hs_ref[...] = spectrum(gath[kind].reshape(RBLK * WORK, BLK))

    def response_products(blocks):
        def one(n):
            at = rows_of(n, OWN)
            tap_row = lax.rem(n, NZ) * OWN
            sig = []
            prev = None
            for m in range(blocks[-1] + 1):
                now = (vs_ref[m, at, :BLK], vs_ref[m, at, BLK:])
                if prev is None:
                    sig.append(now)
                else:
                    sig.append((now[0] - sign * prev[1], now[1] + sign * prev[0]))
                prev = now
            tap = []
            for j in range(blocks[-1] + 1):
                rows = pl.ds(pl.multiple_of(j * WORK + tap_row, OWN), OWN)
                tap.append((hs_ref[rows, :BLK], hs_ref[rows, BLK:]))
            for i in blocks:
                real = imag = None
                for m in range(i + 1):
                    (xr, xi), (hr, hi) = sig[m], tap[i - m]
                    pr = xr * hr - xi * hi
                    pi = xr * hi + xi * hr
                    real = pr if real is None else real + pr
                    imag = pi if imag is None else imag + pi
                q_hi[i, at, :BLK], q_lo[i, at, :BLK] = split(real * (1.0 / BLK))
                q_hi[i, at, BLK:], q_lo[i, at, BLK:] = split(imag * (1.0 / BLK))

        loop(0, BLK // OWN, one)

    pack(0, x_ref)
    pack(1, h1_ref)
    pl.semaphore_wait(barrier, NCTX - 1 + nch - 1)
    loop(1, NCTX, lambda k: in_copy(0, k).start())
    pack(2, g1_ref)
    pack(3, h2_ref)
    loop(1, NCTX, lambda k: in_copy(1, k).start())
    send_response(0, v_ref)
    send_response(1, ri_ref)
    send_response(2, ro_ref)
    loaded(ft_hi, ft_lo, f_hi, f_lo, g2_ref, rd_ref)

    loop(1, NCTX, lambda k: in_copy(0, k).wait_recv())
    share(0, recv_in[1, : RBLK * OWN, :])
    set_taps(recv_in[1])
    conv = owner_convolution(recv_in[0])
    share(1, conv[BLK:].astype(BF16))

    have_response(0)
    for b in range(RBLK):
        vs_ref[b] = spectrum(response(0, b))

    loop(1, NCTX, lambda k: in_copy(1, k).wait_recv())
    share(2, recv_in[3, : RBLK * OWN, :])
    set_taps(recv_in[3])
    gated = (recv_in[2].astype(F32) * conv[:BLK]).astype(BF16)
    conv = owner_convolution(gated)
    share(3, conv[BLK:].astype(BF16))
    back_send[...] = conv[:BLK].astype(BF16)

    shared(0)
    head_spectrum(0)
    response_products(range(RBLK))
    shared(1)
    have_response(1)
    for b in range(RBLK):
        total = tail(1, b) + inverse(q_hi[b], q_lo[b])
        gated = (response(1, b).astype(F32) * total).astype(BF16)
        vs_ref[b] = spectrum(gated)
    shared(2)
    head_spectrum(2)
    response_products(range(RBLK))
    have_response(2)

    lane = lax.broadcasted_iota(jnp.int32, (16, BLK), 1)
    row = lax.broadcasted_iota(jnp.int32, (16, BLK), 0)
    weight = jnp.where(lane // WORK == yy, jnp.broadcast_to(rd_ref[...], (16, BLK)), 0.0)
    weight = weight + pltpu.roll(weight, BLK // 2, 1)
    weight = weight + pltpu.roll(weight, WORK, 1)
    w_hi = weight.astype(BF16).astype(F32)
    w_mid = (weight - w_hi).astype(BF16).astype(F32)
    w_lo = weight - w_hi - w_mid
    term = row // NY
    weight = jnp.where(term == 0, w_hi, jnp.where(term == 1, w_mid, w_lo))
    weight = jnp.where(term < 3, weight, 0.0)
    weight = jnp.where(lax.rem(row, NY) == lane // WORK, weight, 0.0).astype(BF16)

    my_work = rows_of(yy, WORK)
    half = RBLK * BLK // 2

    def out_copy(b, k):
        peer = y_peer(k)
        at = pl.ds(b * half, half)
        return pltpu.make_async_remote_copy(
            src_ref=out_send.at[peer, :, at],
            dst_ref=out_home.at[my_work, at],
            send_sem=out_send_sem.at[b, k],
            recv_sem=out_recv_sem.at[b, k],
            device_id={"ctx": zh * NY + peer},
            device_id_type=MESH,
        )

    for b in range(RBLK):
        vs_ref[b, :, :BLK] = inverse(q_hi[b], q_lo[b])
    shared(3)

    for b in range(RBLK):
        at = slice(b * BLK, (b + 1) * BLK)
        total = tail(3, b) + vs_ref[b, :, :BLK]
        value = (response(2, b).astype(F32) * total).astype(BF16)
        out_send[:, :, at] = value.reshape(NY, WORK, BLK)
        terms = dot(weight, value)
        part = terms[0:4] + terms[4:8] + terms[8:12]
        for n in range(NY):
            part_send[n, 2 * b : 2 * b + 1, :] = part[n : n + 1, :128]
            part_send[n, 2 * b + 1 : 2 * b + 2, :] = part[n : n + 1, 128:]

    def part_copy(k):
        peer = y_peer(k)
        return pltpu.make_async_remote_copy(
            src_ref=part_send.at[peer],
            dst_ref=part_recv.at[yy],
            send_sem=part_send_sem.at[k],
            recv_sem=part_recv_sem.at[k],
            device_id={"ctx": zh * NY + peer},
            device_id_type=MESH,
        )

    loop(1, NY, lambda k: part_copy(k).start())
    for b in range(2):
        loop(1, NY, lambda k: out_copy(b, k).start())
    part_recv[yy] = part_send[yy]
    out_home[my_work, :] = out_send[yy]

    def p_copy(k):
        return pltpu.make_async_remote_copy(
            src_ref=p_send,
            dst_ref=p_recv.at[mc],
            send_sem=p_send_sem.at[k],
            recv_sem=p_recv_sem.at[k],
            device_id={"ch": lax.rem(mc + k, nch)},
            device_id_type=MESH,
        )

    loop(1, NY, lambda k: part_copy(k).wait_recv())
    p_send[...] = part_recv[0] + part_recv[1] + part_recv[2] + part_recv[3]
    if nch > 1:
        loop(1, nch, lambda k: p_copy(k).start())
    p_recv[mc] = p_send[...]

    def back_copy(k):
        peer = ctx_peer(k)
        return pltpu.make_async_remote_copy(
            src_ref=back_send.at[rows_of(peer, OWN), :],
            dst_ref=back_recv.at[my_group, :],
            send_sem=back_send_sem.at[k],
            recv_sem=back_recv_sem.at[k],
            device_id={"ctx": peer},
            device_id_type=MESH,
        )

    loop(1, NCTX, lambda k: back_copy(k).start())
    back_recv[my_group, :] = back_send[mine, :]

    length = len_ref[0]
    stores = []
    for b in range(RBLK):
        at = slice(b * BLK, (b + 1) * BLK)
        if b % 2 == 0:
            loop(1, NY, lambda k: out_copy(b // 2, k).wait_recv())
        token = lax.broadcasted_iota(jnp.int32, (BLK, BLK), 0) + b * BLK
        value = jnp.transpose(out_home[:, at].astype(F32))
        out_ref[at, :] = jnp.where(token < length, value, 0.0).astype(BF16)
        rows = pl.ds(b * BLK, BLK)
        stores.append(
            pltpu.make_async_copy(out_ref.at[rows, :], out_hbm.at[rows, :], store_sem.at[b])
        )
        stores[-1].start()
    loop(1, NCTX, lambda k: back_copy(k).wait_recv())
    po_ref[...] = (
        g2_ref[...].astype(F32) * jnp.transpose(back_recv[...].astype(F32))
    ).astype(BF16)
    stores.append(pltpu.make_async_copy(po_ref, po_hbm, store_sem.at[RBLK]))
    stores[-1].start()

    for stage in range(2):
        loop(1, NCTX, lambda k: in_copy(stage, k).wait_send())
    for which in range(3):
        loop(1, NY, lambda k: resp_copy(which, k).wait_send())
    for kind in range(4):
        loop(1, NZ, lambda k: gz_copy(kind, k).wait_send())
    for b in range(2):
        loop(1, NY, lambda k: out_copy(b, k).wait_send())
    loop(1, NCTX, lambda k: back_copy(k).wait_send())
    loop(1, NY, lambda k: part_copy(k).wait_send())

    if nch > 1:
        loop(1, nch, lambda k: p_copy(k).wait_recv())
    projection = p_recv[0]
    for c in range(1, nch):
        projection = projection + p_recv[c]
    token = (
        lax.broadcasted_iota(jnp.int32, (8, 128), 0) * 128
        + lax.broadcasted_iota(jnp.int32, (8, 128), 1)
    )
    squares = jnp.where(token < length, projection * projection, 0.0)
    sc_ref[0] = jnp.sum(squares) / length.astype(F32)
    if nch > 1:
        loop(1, nch, lambda k: p_copy(k).wait_send())
    for copy in stores:
        copy.wait()


def place(a_ref, b_ref, a_out, b_out, a_buf, b_buf, sem):
    pairs = [(a_ref, a_buf, a_out)]
    for b in range(RBLK):
        rows = pl.ds(b * BLK, BLK)
        pairs.append((b_ref.at[rows, :], b_buf.at[rows, :], b_out.at[rows, :]))
    loads, stores = [], []
    for n, (source, buffer, target) in enumerate(pairs):
        loads.append(pltpu.make_async_copy(source, buffer, sem.at[0, n]))
        stores.append(pltpu.make_async_copy(buffer, target, sem.at[1, n]))
    for copy in loads:
        copy.start()
    for load, store in zip(loads, stores):
        load.wait()
        store.start()
    for copy in stores:
        copy.wait()


def per_device(
    nch,
    prefix_values,
    inner_gate,
    outer_gate,
    inner_filter,
    outer_filter,
    response_values,
    response_inner,
    response_outer,
    lengths,
    readout,
):
    hbm = pl.BlockSpec(memory_space=pl.ANY)
    smem = pl.BlockSpec(memory_space=pltpu.SMEM)
    dma = pltpu.SemaphoreType.DMA
    tokens = RBLK * BLK
    prefix_output, response_output, scores = pl.pallas_call(
        functools.partial(kernel, nch),
        out_shape=(
            jax.ShapeDtypeStruct((BLK, BLK), BF16),
            jax.ShapeDtypeStruct((tokens, BLK), BF16),
            jax.ShapeDtypeStruct((1,), F32),
        ),
        in_specs=[hbm] * 8 + [smem] + [hbm] * 5,
        out_specs=(hbm, hbm, smem),
        scratch_shapes=[
            pltpu.VMEM((BLK, BLK), BF16),
            pltpu.VMEM((tokens, BLK), BF16),
            dma((RBLK + 1,)),
            *[pltpu.VMEM((BLK, BLK), BF16) for _ in range(5)],
            *[pltpu.VMEM((tokens, BLK), BF16) for _ in range(3)],
            pltpu.VMEM((1, BLK), F32),
            *[pltpu.VMEM((2 * BLK, BLK), BF16) for _ in range(2)],
            *[pltpu.VMEM((BLK, 2 * BLK), BF16) for _ in range(2)],
            dma((13,)),
            pltpu.VMEM((4, BLK, BLK), BF16),
            pltpu.VMEM((4, BLK, BLK), BF16),
            pltpu.VMEM((3, BLK, tokens), BF16),
            pltpu.VMEM((3, NY, WORK, tokens), BF16),
            pltpu.VMEM((NCTX + 1, OWN, BLK), F32),
            pltpu.VMEM((NCTX + 1, OWN, BLK), F32),
            pltpu.VMEM((NCTX, OWN, BLK), F32),
            pltpu.VMEM((NCTX, OWN, BLK), F32),
            pltpu.VMEM((NOUT * OWN, 2 * BLK), F32),
            pltpu.VMEM((4, RBLK, NZ, OWN, BLK), BF16),
            pltpu.VMEM((BLK, BLK), BF16),
            pltpu.VMEM((BLK, BLK), BF16),
            pltpu.VMEM((RBLK, BLK, 2 * BLK), F32),
            pltpu.VMEM((RBLK * WORK, 2 * BLK), F32),
            pltpu.VMEM((RBLK, BLK, 2 * BLK), BF16),
            pltpu.VMEM((RBLK, BLK, 2 * BLK), BF16),
            pltpu.VMEM((NY, WORK, tokens), BF16),
            pltpu.VMEM((BLK, tokens), BF16),
            pltpu.VMEM((NY, 8, 128), F32),
            pltpu.VMEM((NY, 8, 128), F32),
            pltpu.VMEM((8, 128), F32),
            pltpu.VMEM((nch, 8, 128), F32),
            dma((2, NCTX)),
            dma((2, NCTX)),
            dma((3, NY)),
            dma((3, NY)),
            dma((4, NZ)),
            dma((4, NZ)),
            dma((NCTX,)),
            dma((NCTX,)),
            dma((2, NY)),
            dma((2, NY)),
            dma((NY,)),
            dma((NY,)),
            dma((nch,)),
            dma((nch,)),
        ],
        compiler_params=pltpu.CompilerParams(
            collective_id=0, has_side_effects=True, vmem_limit_bytes=60 * 1024 * 1024
        ),
        cost_estimate=pl.CostEstimate(
            flops=8_000_000_000, bytes_accessed=5_000_000, transcendentals=0
        ),
        name="gated_convolutions",
    )(
        prefix_values,
        inner_gate,
        outer_gate,
        inner_filter,
        outer_filter,
        response_values.reshape(tokens, BLK),
        response_inner.reshape(tokens, BLK),
        response_outer.reshape(tokens, BLK),
        lengths,
        readout.reshape(1, BLK),
        *[jnp.asarray(t) for t in dft_tables()],
    )
    prefix_output, response_output = pl.pallas_call(
        place,
        out_shape=(
            jax.ShapeDtypeStruct((BLK, BLK), BF16),
            jax.ShapeDtypeStruct((tokens, BLK), BF16),
        ),
        in_specs=[hbm] * 2,
        out_specs=(hbm, hbm),
        scratch_shapes=[
            pltpu.VMEM((BLK, BLK), BF16),
            pltpu.VMEM((tokens, BLK), BF16),
            dma((2, RBLK + 1)),
        ],
        compiler_params=pltpu.CompilerParams(vmem_limit_bytes=60 * 1024 * 1024),
        name="place_outputs",
    )(prefix_output, response_output)
    return prefix_output, response_output.reshape(1, tokens, BLK), scores


def solution(mesh):
    in_specs = (
        P("ctx", "ch"),
        P("ctx", "ch"),
        P("ctx", "ch"),
        P("ctx", "ch"),
        P("ctx", "ch"),
        P("ctx", None, "ch"),
        P("ctx", None, "ch"),
        P("ctx", None, "ch"),
        P("ctx"),
        P("ch"),
    )
    out_specs = (P("ctx", "ch"), P("ctx", None, "ch"), P("ctx"))
    return jax.shard_map(
        functools.partial(per_device, mesh.shape["ch"]),
        mesh=mesh,
        in_specs=in_specs,
        out_specs=out_specs,
        check_vma=False,
    )
```
